512 devices in a mesh: row: 32 (over y, z_hi, core), col: 16 (over x, z_lo).
Axes of the slice: x: 4, y: 8, z: 8 (z_hi: 2, z_lo: 4; z = z_hi * 4 + z_lo), core: 2. Of those that a mesh axis runs over, the one named last changes fastest.
Arguments:
- precision_matrix: float32 [12288, 12288], P('row', 'col'), may hold values from -1 to 3, as said below
- sample_rows: float32 [12288, 1024], P('row'), may hold values from -6 to 6
Outputs:
- updated_matrix: float32 [12288, 12288], P('row', 'col')
- next_product: float32 [12288, 1024], P(('row', 'col'))
The draws below stay inside these ranges and needn't reach their ends.
Inputs may be any that keep to these rules, and one draw needn't show every extreme that they name: `precision_matrix`: Symmetric; diagonal entries between 1 and 3.
All inputs are finite; a program needn't handle non-finite values.
Results may differ from the reference program's by a relative error of at most 0.0003.
Values sent between devices are 32-bit elements; how exact they have to be, the bound alone decides.
No kernel may reach another device: no remote copies, remote signals or barrier semaphores. Data moves between devices by JAX's collectives and lax.ppermute only.
A program may use at most 64 MiB of HBM per device.

```python
import jax
import jax.numpy as jnp
from jax import lax

P_SIZE = 12288
SAMPLES = 1024


def draw_precision_matrix(key, part):
    first, second = jax.random.split(key, 2)
    normal = jax.random.normal(first, (P_SIZE, P_SIZE), jnp.float32)
    offdiag = 0.01 * 0.7071 * (normal + normal.T)
    offdiag = jnp.clip(offdiag, -0.9, 0.9)
    diagonal = jax.random.uniform(second, (P_SIZE,), jnp.float32, 1.0, 3.0)
    eye = jnp.eye(P_SIZE, dtype=jnp.float32)
    return offdiag * (1.0 - eye) + eye * diagonal[None, :]


def block_levels(own_key, shape, cuts, smallest, high):
    loudness, own = 1.0, jax.random.fold_in(own_key, 6)
    for dim, blocks in cuts:
        draws = jnp.exp(jax.random.uniform(jax.random.fold_in(own, dim), (blocks,), jnp.float32, smallest / len(cuts), high / len(cuts)))
        loudness = loudness * jnp.repeat(draws, shape[dim] // blocks).reshape([-1 if axis == dim else 1 for axis in range(len(shape))])
    return loudness


def scatter_about(own_key, dims, deviation, reach, shards=(), kind=jnp.bfloat16):
    entries = jax.random.normal(own_key, dims, jnp.float32) * deviation
    if len(shards) > 0:
        entries = block_levels(own_key, dims, shards, -0.22, 0.18) * entries
    return jnp.clip(entries, min=-reach, max=reach).astype(kind)


def setup_inputs(seed: int = 0) -> dict:
    arg_keys = jax.random.split(jax.random.key(seed), 3)
    precision_matrix = draw_precision_matrix(jax.random.fold_in(arg_keys[2], 71), 0)
    sample_rows = scatter_about(arg_keys[1], (P_SIZE, SAMPLES), 1.0, 6.0, ((0, 32),), jnp.float32)
    return {"precision_matrix": precision_matrix, "sample_rows": sample_rows}


step_length = 0.5
penalty = 0.02


def reference(precision_matrix, sample_rows):
    highest = lax.Precision.HIGHEST
    product = jnp.dot(precision_matrix, sample_rows, precision=highest, preferred_element_type=jnp.float32)
    cross = jnp.dot(product, sample_rows.T, precision=highest, preferred_element_type=jnp.float32) / SAMPLES
    diagonal = jnp.diagonal(precision_matrix)
    gradient = 0.5 * (cross + cross.T)
    gradient = gradient - jnp.diag(1.0 / diagonal)
    moved = precision_matrix - step_length * gradient
    shrunk = jnp.sign(moved) * jnp.maximum(jnp.abs(moved) - step_length * penalty, 0.0)
    on_diagonal = jnp.eye(P_SIZE, dtype=jnp.bool_)
    updated = jnp.where(on_diagonal, moved, shrunk)
    next_product = jnp.dot(updated, sample_rows, precision=highest, preferred_element_type=jnp.float32)
    return updated, next_product
```

```python
import jax
import jax.numpy as jnp
import numpy as np
from jax import lax
from jax.sharding import Mesh, PartitionSpec as P

step_length = 0.5
penalty = 0.02

PARTS = {"y": 8, "zh": 2, "c": 2, "x": 4, "zl": 4}
AXES = tuple(PARTS)
SIZES = tuple(PARTS.values())
PREC = lax.Precision.HIGH


def permute(v, move):
    count = int(np.prod(SIZES))
    pairs = []
    for k in range(count):
        at = [int(p) for p in np.unravel_index(k, SIZES)]
        pairs.append((k, int(np.ravel_multi_index(move(*at), SIZES))))
    return lax.ppermute(v, AXES, pairs)


def swap_core(v):
    return permute(v, lambda y, zh, c, x, zl: (y, zh, 1 - c, x, zl))


def swap_zh(v):
    return permute(v, lambda y, zh, c, x, zl: (y, 1 - zh, c, x, zl))


def transpose_chips(v):
    def move(y, zh, c, x, zl):
        i, j = 2 * y + zh, 4 * x + zl
        return (j // 2, j % 2, c, i // 4, i % 4)

    return permute(v, move)


def transpose_shifted(v):
    def move(y, zh, c, x, zl):
        i, j = 2 * ((y - c) % 8) + zh, 4 * x + zl
        return (j // 2, j % 2, c, i // 4, i % 4)

    return permute(v, move)


def pair_swap(v, axis, odd_step):
    at = AXES.index(axis)
    n = PARTS[axis]

    def move(*place):
        place = list(place)
        parity = (place[at] - place[2]) % 2
        step = 1 if parity == odd_step else -1
        place[at] = (place[at] + step) % n
        return tuple(place)

    return permute(v, move)


def take(v, start, size):
    return lax.dynamic_slice_in_dim(v, start, size, 0)


def put(v, part, start):
    return lax.dynamic_update_slice_in_dim(v, part, start, 0)


def sum_ring8(v, y, c):
    b = v.shape[0] // 8
    p = (y - c) % 8
    k, odd = p // 2, p % 2

    def pair(j):
        return take(v, (j % 4) * (2 * b), 2 * b)

    near = jnp.where(odd == 0, k + 1, k - 1)
    other = jnp.where(odd == 0, k - 1, k + 1)
    got = pair_swap(pair(k + 2), "y", 1)
    got = pair_swap(pair(near) + got, "y", 0)
    got = pair_swap(pair(other) + got, "y", 1)
    mine = pair(k) + got
    got = pair_swap(take(mine, (1 - odd) * b, b), "y", 0)
    return take(mine, odd * b, b) + got


def gather_ring8(v, y, c):
    b = v.shape[0]
    p = (y - c) % 8
    k, odd = p // 2, p % 2
    got = pair_swap(v, "y", 0)
    own = put(put(jnp.zeros((2 * b, *v.shape[1:]), v.dtype), v, odd * b), got, (1 - odd) * b)
    second = pair_swap(own, "y", 1)
    third = pair_swap(second, "y", 0)
    fourth = pair_swap(third, "y", 1)
    out = jnp.zeros((8 * b, *v.shape[1:]), v.dtype)
    near = jnp.where(odd == 0, k + 1, k - 1)
    other = jnp.where(odd == 0, k - 1, k + 1)
    for part, j in ((own, k), (second, other), (third, near), (fourth, k + 2)):
        out = put(out, part, (j % 4) * (2 * b))
    return out


def gather_ring4(v, x, c):
    b = v.shape[0]
    p = (x - c) % 4
    odd = p % 2
    first = pair_swap(v, "x", 0)
    second = pair_swap(jnp.concatenate([v, first]), "x", 1)
    out = jnp.zeros((4 * b, *v.shape[1:]), v.dtype)
    partner = jnp.where(odd == 0, x + 1, x - 1)
    far = jnp.where(odd == 0, x - 1, x + 1)
    for part, j in ((v, x), (first, partner), (second[:b], far), (second[b:], x + 2)):
        out = put(out, part, (j % 4) * b)
    return out


def scatter_sum(v, axis):
    n = PARTS[axis]
    parts = lax.all_to_all(v.reshape(n, -1, v.shape[1]), axis, 0, 0, tiled=True)
    return jnp.sum(parts, axis=0)


def both_cores(v, c):
    other = swap_core(v)
    out = jnp.zeros((2 * v.shape[0], *v.shape[1:]), v.dtype)
    return put(put(out, v, c * v.shape[0]), other, (1 - c) * v.shape[0])


def dot(a, b, contract):
    return lax.dot_general(
        a, b, (contract, ((), ())), precision=PREC, preferred_element_type=jnp.float32
    )


def on_device(precision_matrix, sample_rows):
    row_count, col_count = precision_matrix.shape
    samples = sample_rows.shape[1]
    y, zh, c, x, zl = (lax.axis_index(a) for a in AXES)
    row_chip, col_chip = 2 * y + zh, 4 * x + zl
    half = col_count // 2
    block = half // 8

    slices = transpose_chips(take(sample_rows, (col_chip // 2) * block, block))

    def partial_rows(h):
        cols = lax.dynamic_slice_in_dim(precision_matrix, h * half, half, 1)
        return dot(cols, sample_rows, ((0,), (0,)))

    got = swap_core(partial_rows(1 - c))
    partial_value = partial_rows(c) + got

    data_half = lax.all_gather(slices, "y", axis=0, tiled=True)

    product = sum_ring8(partial_value, y, c)
    product = product + swap_zh(product)

    own = transpose_shifted(take(product, zh * (block // 2), block // 2))
    own = lax.all_gather(own, "zl", axis=0, tiled=True)
    product_rows = gather_ring4(own, x, c)
    product_cols = both_cores(gather_ring8(product, y, c), c)
    data_cols = both_cores(data_half, c)

    last = ((1,), (1,))
    cross = dot(sample_rows, product_cols, last) + dot(product_rows, data_cols, last)
    gradient = cross * (0.5 / samples)

    global_rows = (2 * row_chip + c) * row_count + lax.broadcasted_iota(
        jnp.int32, (row_count, col_count), 0
    )
    global_cols = col_chip * col_count + lax.broadcasted_iota(
        jnp.int32, (row_count, col_count), 1
    )
    on_diagonal = global_rows == global_cols
    inverse = 1.0 / jnp.where(on_diagonal, precision_matrix, 1.0)
    gradient = gradient - jnp.where(on_diagonal, inverse, 0.0)
    moved = precision_matrix - step_length * gradient
    shrunk = jnp.sign(moved) * jnp.maximum(jnp.abs(moved) - step_length * penalty, 0.0)
    updated = jnp.where(on_diagonal, moved, shrunk)
    next_partial = dot(updated, data_cols, ((1,), (0,)))
    next_product = scatter_sum(scatter_sum(next_partial, "x"), "zl")
    return updated, next_product


def solution(mesh):
    parts = Mesh(mesh.devices.reshape(SIZES), AXES)
    row, col = ("y", "zh", "c"), ("x", "zl")
    return jax.shard_map(
        on_device,
        mesh=parts,
        in_specs=(P(row, col), P(row, None)),
        out_specs=(P(row, col), P(row + col, None)),
        check_vma=False,
    )
```

```python
import jax
import jax.numpy as jnp
import numpy as np
from jax import lax
from jax.sharding import Mesh, PartitionSpec as P

step_length = 0.5
penalty = 0.02

PARTS = {"y": 8, "zh": 2, "c": 2, "x": 4, "zl": 4}
AXES = tuple(PARTS)
SIZES = tuple(PARTS.values())
PREC = lax.Precision.HIGH


def permute(v, move):
    count = int(np.prod(SIZES))
    pairs = []
    for k in range(count):
        at = [int(p) for p in np.unravel_index(k, SIZES)]
        pairs.append((k, int(np.ravel_multi_index(move(*at), SIZES))))
    return lax.ppermute(v, AXES, pairs)


def swap_core(v):
    return permute(v, lambda y, zh, c, x, zl: (y, zh, 1 - c, x, zl))


def swap_zh(v):
    return permute(v, lambda y, zh, c, x, zl: (y, 1 - zh, c, x, zl))


def data_target(y, zh, x, zl):
    return (2 * x + zl // 2 - y) % 8, zl % 2


def transpose_data(v):
    def move(y, zh, c, x, zl):
        row_y, row_zh = data_target(y, zh, x, zl)
        return (row_y, row_zh, c, y // 2, 2 * (y % 2) + zh)

    return permute(v, move)


def transpose_in_plane(v):
    def move(y, zh, c, x, zl):
        p = (y - c) % 8
        return (y, zl % 2, c, (p // 2 + x) % 4, 2 * (p % 2 ^ zl // 2) + zh)

    return permute(v, move)


def transpose_along_y(v):
    def move(y, zh, c, x, zl):
        p = (y - c) % 8
        return (2 * ((x - p // 2) % 4) + (p % 2 ^ zl // 2), zh, c, x, zl)

    return permute(v, move)


def pair_swap(v, axis, odd_step, flip=0):
    at = AXES.index(axis)
    n = PARTS[axis]

    def move(*place):
        place = list(place)
        parity = (place[at] - (place[2] ^ flip)) % 2
        step = 1 if parity == odd_step else -1
        place[at] = (place[at] + step) % n
        return tuple(place)

    return permute(v, move)


def take(v, start, size):
    return lax.dynamic_slice_in_dim(v, start, size, 0)


def put(v, part, start):
    return lax.dynamic_update_slice_in_dim(v, part, start, 0)


def in_pair(own, got, odd):
    return jnp.where(odd == 0, jnp.concatenate([own, got]), jnp.concatenate([got, own]))


def place_pairs(parts, k, odd):
    near = jnp.where(odd == 0, k + 1, k - 1)
    other = jnp.where(odd == 0, k - 1, k + 1)
    rows = parts[0].shape[0]
    out = jnp.zeros((4 * rows, *parts[0].shape[1:]), parts[0].dtype)
    for part, j in zip(parts, (k, other, near, k + 2)):
        out = put(out, part, (j % 4) * rows)
    return out


def scatter_sum(v, axis):
    n = PARTS[axis]
    parts = lax.all_to_all(v.reshape(n, -1, v.shape[1]), axis, 0, 0, tiled=True)
    return jnp.sum(parts, axis=0)


def both_cores(v, c):
    other = swap_core(v)
    out = jnp.zeros((2 * v.shape[0], *v.shape[1:]), v.dtype)
    return put(put(out, v, c * v.shape[0]), other, (1 - c) * v.shape[0])


def together(*parts):
    return lax.optimization_barrier(parts)


def dot(a, b, contract):
    return lax.dot_general(
        a, b, (contract, ((), ())), precision=PREC, preferred_element_type=jnp.float32
    )


def on_device(precision_matrix, sample_rows):
    row_count, col_count = precision_matrix.shape
    samples = sample_rows.shape[1]
    y, zh, c, x, zl = (lax.axis_index(a) for a in AXES)
    row_chip, col_chip = 2 * y + zh, 4 * x + zl
    half = col_count // 2
    block = half // 8
    place = (y - c) % 8
    pair, odd = place // 2, place % 2

    target, _ = data_target(y, zh, x, zl)
    share = take(sample_rows, target * block, block)

    def partial_rows(h):
        cols = lax.dynamic_slice_in_dim(precision_matrix, h * half, half, 1)
        return dot(cols, sample_rows, ((0,), (0,)))

    got = swap_core(partial_rows(1 - c))
    (kept,) = together(partial_rows(c))

    def sums(at):
        start = (at % 4) * (2 * block)
        return take(kept, start, 2 * block) + take(got, start, 2 * block)

    near = jnp.where(odd == 0, pair + 1, pair - 1)
    other = jnp.where(odd == 0, pair - 1, pair + 1)
    sending, share = together(sums(pair + 2), share)
    passed = pair_swap(sending, "y", 1)
    data = transpose_data(share)
    passed = pair_swap(sums(near) + passed, "y", 0)
    sending, data = together(sums(other) + passed, data)
    data_half = lax.all_gather(data, "y", axis=0, tiled=True)
    passed = pair_swap(sending, "y", 1)
    mine = sums(pair) + passed
    passed = pair_swap(take(mine, (1 - odd) * block, block), "y", 0)
    product = take(mine, odd * block, block) + passed
    product = product + swap_zh(product)

    own = take(product, zh * (block // 2), block // 2)
    product, own = together(product, own)
    own = transpose_in_plane(own)
    pair0 = in_pair(product, pair_swap(product, "y", 0), odd)
    pair0, own = together(pair0, own)
    own = transpose_along_y(own)
    pair1 = pair_swap(pair0, "y", 1)
    pair1, own = together(pair1, own)
    pair2 = pair_swap(pair1, "y", 0)
    own = lax.all_gather(own, "zl", axis=0, tiled=True)
    own = in_pair(own[:block], own[block:], row_chip // 2 % 2)
    pair2, own, data_half = together(pair2, own, data_half)
    pair3 = pair_swap(pair2, "y", 1)
    x_odd = (x - c) % 2
    rows0 = in_pair(own, pair_swap(own, "x", 0), x_odd)
    data_cols = both_cores(data_half, c)
    pair3, rows0 = together(pair3, rows0)
    rows1 = pair_swap(rows0, "x", 1)
    product_cols = both_cores(place_pairs([pair0, pair1, pair2, pair3], pair, odd), c)
    product_rows = jnp.zeros_like(sample_rows)
    first = x - x_odd - row_chip // 4
    for part, at in (
        (rows0[: 2 * block], first),
        (rows0[2 * block :], first + 1),
        (rows1[: 2 * block], first + 2),
        (rows1[2 * block :], first + 3),
    ):
        product_rows = put(product_rows, part, (at % 4) * (2 * block))

    last = ((1,), (1,))
    cross = dot(sample_rows, product_cols, last) + dot(product_rows, data_cols, last)
    gradient = cross * (0.5 / samples)

    global_rows = (2 * row_chip + c) * row_count + lax.broadcasted_iota(
        jnp.int32, (row_count, col_count), 0
    )
    global_cols = col_chip * col_count + lax.broadcasted_iota(
        jnp.int32, (row_count, col_count), 1
    )
    on_diagonal = global_rows == global_cols
    inverse = 1.0 / jnp.where(on_diagonal, precision_matrix, 1.0)
    gradient = gradient - jnp.where(on_diagonal, inverse, 0.0)
    moved = precision_matrix - step_length * gradient
    shrunk = jnp.sign(moved) * jnp.maximum(jnp.abs(moved) - step_length * penalty, 0.0)
    updated = jnp.where(on_diagonal, moved, shrunk)
    next_partial = dot(updated, data_cols, ((1,), (0,)))
    next_product = scatter_sum(scatter_sum(next_partial, "x"), "zl")
    return updated, next_product


def solution(mesh):
    parts = Mesh(mesh.devices.reshape(SIZES), AXES)
    row, col = ("y", "zh", "c"), ("x", "zl")
    return jax.shard_map(
        on_device,
        mesh=parts,
        in_specs=(P(row, col), P(row, None)),
        out_specs=(P(row, col), P(row + col, None)),
        check_vma=False,
    )
```

```python
import jax
import jax.numpy as jnp
import numpy as np
from jax import lax
from jax.sharding import Mesh, PartitionSpec as P

step_length = 0.5
penalty = 0.02

PARTS = {"y": 8, "zh": 2, "c": 2, "x": 4, "zl": 4}
AXES = tuple(PARTS)
SIZES = tuple(PARTS.values())
PREC = lax.Precision.HIGH


def permute(v, move):
    count = int(np.prod(SIZES))
    pairs = []
    for k in range(count):
        at = [int(p) for p in np.unravel_index(k, SIZES)]
        pairs.append((k, int(np.ravel_multi_index(move(*at), SIZES))))
    return lax.ppermute(v, AXES, pairs)


def swap_core(v):
    return permute(v, lambda y, zh, c, x, zl: (y, zh, 1 - c, x, zl))


def swap_zh(v):
    return permute(v, lambda y, zh, c, x, zl: (y, 1 - zh, c, x, zl))


def data_target(y, zh, x, zl):
    return (2 * x + zl // 2 - y) % 8, zl % 2


def transpose_data(v):
    def move(y, zh, c, x, zl):
        row_y, row_zh = data_target(y, zh, x, zl)
        return (row_y, row_zh, c, y // 2, 2 * (y % 2) + zh)

    return permute(v, move)


def transpose_in_plane(v):
    def move(y, zh, c, x, zl):
        p = (y - c) % 8
        return (y, zl % 2, c, (p // 2 + x) % 4, 2 * (p % 2 ^ zl // 2) + zh)

    return permute(v, move)


def transpose_along_y(v):
    def move(y, zh, c, x, zl):
        p = (y - c) % 8
        return (2 * ((x - p // 2) % 4) + (p % 2 ^ zl // 2), zh, c, x, zl)

    return permute(v, move)


def pair_swap(v, axis, odd_step, flip=0):
    at = AXES.index(axis)
    n = PARTS[axis]

    def move(*place):
        place = list(place)
        parity = (place[at] - (place[2] ^ flip)) % 2
        step = 1 if parity == odd_step else -1
        place[at] = (place[at] + step) % n
        return tuple(place)

    return permute(v, move)


def take(v, start, size):
    return lax.dynamic_slice_in_dim(v, start, size, 0)


def put(v, part, start):
    return lax.dynamic_update_slice_in_dim(v, part, start, 0)


def in_pair(own, got, odd):
    return jnp.where(odd == 0, jnp.concatenate([own, got]), jnp.concatenate([got, own]))


def scatter_sum(v, axis):
    n = PARTS[axis]
    parts = lax.all_to_all(v.reshape(n, -1, v.shape[1]), axis, 0, 0, tiled=True)
    return jnp.sum(parts, axis=0)


def both_cores(v, c):
    other = swap_core(v)
    out = jnp.zeros((2 * v.shape[0], *v.shape[1:]), v.dtype)
    return put(put(out, v, c * v.shape[0]), other, (1 - c) * v.shape[0])


def together(*parts):
    return lax.optimization_barrier(parts)


def dot(a, b, contract):
    return lax.dot_general(
        a, b, (contract, ((), ())), precision=PREC, preferred_element_type=jnp.float32
    )


def on_device(precision_matrix, sample_rows):
    row_count, col_count = precision_matrix.shape
    samples = sample_rows.shape[1]
    y, zh, c, x, zl = (lax.axis_index(a) for a in AXES)
    row_chip, col_chip = 2 * y + zh, 4 * x + zl
    half = col_count // 2
    block = half // 8
    place = (y - c) % 8
    pair, odd = place // 2, place % 2

    target, _ = data_target(y, zh, x, zl)
    share = take(sample_rows, target * block, block)

    def partial_rows(h):
        cols = lax.dynamic_slice_in_dim(precision_matrix, h * half, half, 1)
        return dot(cols, sample_rows, ((0,), (0,)))

    got = swap_core(partial_rows(1 - c))
    (kept,) = together(partial_rows(c))

    def sums(at):
        start = (at % 4) * (2 * block)
        return take(kept, start, 2 * block) + take(got, start, 2 * block)

    near = jnp.where(odd == 0, pair + 1, pair - 1)
    other = jnp.where(odd == 0, pair - 1, pair + 1)
    sending, share = together(sums(pair + 2), share)
    passed = pair_swap(sending, "y", 1)
    data = transpose_data(share)
    passed = pair_swap(sums(near) + passed, "y", 0)
    sending, data = together(sums(other) + passed, data)
    data_half = lax.all_gather(data, "y", axis=0, tiled=True)
    passed = pair_swap(sending, "y", 1)
    mine = sums(pair) + passed
    passed = pair_swap(take(mine, (1 - odd) * block, block), "y", 0)
    product = take(mine, odd * block, block) + passed
    product = product + swap_zh(product)

    own = take(product, zh * (block // 2), block // 2)
    product_half = lax.all_gather(product, "y", axis=0, tiled=True)
    own = transpose_along_y(transpose_in_plane(own))
    own = lax.all_gather(own, "zl", axis=0, tiled=True)
    own = in_pair(own[:block], own[block:], row_chip // 2 % 2)
    own, data_half = together(own, data_half)
    x_odd = (x - c) % 2
    rows0 = in_pair(own, pair_swap(own, "x", 0), x_odd)
    data_cols = both_cores(data_half, c)
    rows1 = pair_swap(rows0, "x", 1)
    shifted = jnp.concatenate([product_half[block:], product_half[:block]])
    product_cols = both_cores(jnp.where(c == 0, product_half, shifted), c)
    product_rows = jnp.zeros_like(sample_rows)
    first = x - x_odd - row_chip // 4
    for part, at in (
        (rows0[: 2 * block], first),
        (rows0[2 * block :], first + 1),
        (rows1[: 2 * block], first + 2),
        (rows1[2 * block :], first + 3),
    ):
        product_rows = put(product_rows, part, (at % 4) * (2 * block))

    last = ((1,), (1,))
    cross = dot(sample_rows, product_cols, last) + dot(product_rows, data_cols, last)
    gradient = cross * (0.5 / samples)

    global_rows = (2 * row_chip + c) * row_count + lax.broadcasted_iota(
        jnp.int32, (row_count, col_count), 0
    )
    global_cols = col_chip * col_count + lax.broadcasted_iota(
        jnp.int32, (row_count, col_count), 1
    )
    on_diagonal = global_rows == global_cols
    inverse = 1.0 / jnp.where(on_diagonal, precision_matrix, 1.0)
    gradient = gradient - jnp.where(on_diagonal, inverse, 0.0)
    moved = precision_matrix - step_length * gradient
    shrunk = jnp.sign(moved) * jnp.maximum(jnp.abs(moved) - step_length * penalty, 0.0)
    updated = jnp.where(on_diagonal, moved, shrunk)
    next_partial = dot(updated, data_cols, ((1,), (0,)))
    next_product = scatter_sum(scatter_sum(next_partial, "x"), "zl")
    return updated, next_product


def solution(mesh):
    parts = Mesh(mesh.devices.reshape(SIZES), AXES)
    row, col = ("y", "zh", "c"), ("x", "zl")
    return jax.shard_map(
        on_device,
        mesh=parts,
        in_specs=(P(row, col), P(row, None)),
        out_specs=(P(row, col), P(row + col, None)),
        check_vma=False,
    )
```

```python
import jax
import jax.numpy as jnp
import numpy as np
from jax import lax
from jax.sharding import Mesh, PartitionSpec as P

step_length = 0.5
penalty = 0.02

PARTS = {"y": 8, "zh": 2, "c": 2, "x": 4, "zl": 4}
AXES = tuple(PARTS)
SIZES = tuple(PARTS.values())
PREC = lax.Precision.HIGH


def permute(v, move):
    count = int(np.prod(SIZES))
    pairs = []
    for k in range(count):
        at = [int(p) for p in np.unravel_index(k, SIZES)]
        pairs.append((k, int(np.ravel_multi_index(move(*at), SIZES))))
    return lax.ppermute(v, AXES, pairs)


def swap_core(v):
    return permute(v, lambda y, zh, c, x, zl: (y, zh, 1 - c, x, zl))


def swap_zh(v):
    return permute(v, lambda y, zh, c, x, zl: (y, 1 - zh, c, x, zl))


def data_target(y, zh, x, zl):
    return (2 * x + zl // 2 - y) % 8, zl % 2


def transpose_data(v):
    def move(y, zh, c, x, zl):
        row_y, row_zh = data_target(y, zh, x, zl)
        return (row_y, row_zh, c, y // 2, 2 * (y % 2) + zh)

    return permute(v, move)


def transpose_in_plane(v):
    def move(y, zh, c, x, zl):
        p = (y - c) % 8
        return (y, zl % 2, c, (p // 2 + x) % 4, 2 * (p % 2 ^ zl // 2) + zh)

    return permute(v, move)


def transpose_along_y(v):
    def move(y, zh, c, x, zl):
        p = (y - c) % 8
        return (2 * ((x - p // 2) % 4) + (p % 2 ^ zl // 2), zh, c, x, zl)

    return permute(v, move)


def pair_swap(v, axis, odd_step, flip=0):
    at = AXES.index(axis)
    n = PARTS[axis]

    def move(*place):
        place = list(place)
        parity = (place[at] - (place[2] ^ flip)) % 2
        step = 1 if parity == odd_step else -1
        place[at] = (place[at] + step) % n
        return tuple(place)

    return permute(v, move)


def take(v, start, size):
    return lax.dynamic_slice_in_dim(v, start, size, 0)


def put(v, part, start):
    return lax.dynamic_update_slice_in_dim(v, part, start, 0)


def in_pair(own, got, odd):
    return jnp.where(odd == 0, jnp.concatenate([own, got]), jnp.concatenate([got, own]))


def scatter_sum(v, axis):
    n = PARTS[axis]
    parts = lax.all_to_all(v.reshape(n, -1, v.shape[1]), axis, 0, 0, tiled=True)
    return jnp.sum(parts, axis=0)


def both_cores(v, c):
    other = swap_core(v)
    out = jnp.zeros((2 * v.shape[0], *v.shape[1:]), v.dtype)
    return put(put(out, v, c * v.shape[0]), other, (1 - c) * v.shape[0])


def together(*parts):
    return lax.optimization_barrier(parts)


def dot(a, b, contract):
    return lax.dot_general(
        a, b, (contract, ((), ())), precision=PREC, preferred_element_type=jnp.float32
    )


def on_device(precision_matrix, sample_rows):
    row_count, col_count = precision_matrix.shape
    samples = sample_rows.shape[1]
    y, zh, c, x, zl = (lax.axis_index(a) for a in AXES)
    row_chip, col_chip = 2 * y + zh, 4 * x + zl
    half = col_count // 2
    block = half // 8
    place = (y - c) % 8
    pair, odd = place // 2, place % 2

    target, _ = data_target(y, zh, x, zl)
    share = take(sample_rows, target * block, block)

    def partial_rows(h):
        cols = lax.dynamic_slice_in_dim(precision_matrix, h * half, half, 1)
        return dot(cols, sample_rows, ((0,), (0,)))

    got = swap_core(partial_rows(1 - c))
    (kept,) = together(partial_rows(c))

    def sums(at):
        start = (at % 4) * (2 * block)
        return take(kept, start, 2 * block) + take(got, start, 2 * block)

    near = jnp.where(odd == 0, pair + 1, pair - 1)
    other = jnp.where(odd == 0, pair - 1, pair + 1)
    sending, share = together(sums(pair + 2), share)
    passed = pair_swap(sending, "y", 1)
    data = transpose_data(share)
    passed = pair_swap(sums(near) + passed, "y", 0)
    sending = sums(other) + passed
    passed = pair_swap(sending, "y", 1)
    mine = sums(pair) + passed
    passed = pair_swap(take(mine, (1 - odd) * block, block), "y", 0)
    product = take(mine, odd * block, block) + passed
    product = product + swap_zh(product)

    own = take(product, zh * (block // 2), block // 2)
    pieces = lax.all_gather(jnp.stack([product, data]), "y", axis=1, tiled=True)
    own = transpose_along_y(transpose_in_plane(own))
    own = lax.all_gather(own, "zl", axis=0, tiled=True)
    own = in_pair(own[:block], own[block:], row_chip // 2 % 2)
    x_odd = (x - c) % 2
    rows0 = in_pair(own, pair_swap(own, "x", 0), x_odd)
    rows1 = pair_swap(rows0, "x", 1)
    pieces, _ = together(pieces, rows0)
    data_cols = both_cores(pieces[1], c)
    product_half = pieces[0]
    shifted = jnp.concatenate([product_half[block:], product_half[:block]])
    product_cols = both_cores(jnp.where(c == 0, product_half, shifted), c)
    product_rows = jnp.zeros_like(sample_rows)
    first = x - x_odd - row_chip // 4
    for part, at in (
        (rows0[: 2 * block], first),
        (rows0[2 * block :], first + 1),
        (rows1[: 2 * block], first + 2),
        (rows1[2 * block :], first + 3),
    ):
        product_rows = put(product_rows, part, (at % 4) * (2 * block))

    last = ((1,), (1,))
    cross = dot(sample_rows, product_cols, last) + dot(product_rows, data_cols, last)
    gradient = cross * (0.5 / samples)

    global_rows = (2 * row_chip + c) * row_count + lax.broadcasted_iota(
        jnp.int32, (row_count, col_count), 0
    )
    global_cols = col_chip * col_count + lax.broadcasted_iota(
        jnp.int32, (row_count, col_count), 1
    )
    on_diagonal = global_rows == global_cols
    inverse = 1.0 / jnp.where(on_diagonal, precision_matrix, 1.0)
    gradient = gradient - jnp.where(on_diagonal, inverse, 0.0)
    moved = precision_matrix - step_length * gradient
    shrunk = jnp.sign(moved) * jnp.maximum(jnp.abs(moved) - step_length * penalty, 0.0)
    updated = jnp.where(on_diagonal, moved, shrunk)
    next_partial = dot(updated, data_cols, ((1,), (0,)))
    next_product = scatter_sum(scatter_sum(next_partial, "x"), "zl")
    return updated, next_product


def solution(mesh):
    parts = Mesh(mesh.devices.reshape(SIZES), AXES)
    row, col = ("y", "zh", "c"), ("x", "zl")
    return jax.shard_map(
        on_device,
        mesh=parts,
        in_specs=(P(row, col), P(row, None)),
        out_specs=(P(row, col), P(row + col, None)),
        check_vma=False,
    )
```

```python
import jax
import jax.numpy as jnp
import numpy as np
from jax import lax
from jax.sharding import Mesh, PartitionSpec as P

step_length = 0.5
penalty = 0.02

PARTS = {"y": 8, "zh": 2, "c": 2, "x": 4, "zl": 4}
AXES = tuple(PARTS)
SIZES = tuple(PARTS.values())
PREC = lax.Precision.HIGH


def permute(v, move):
    count = int(np.prod(SIZES))
    pairs = []
    for k in range(count):
        at = [int(p) for p in np.unravel_index(k, SIZES)]
        pairs.append((k, int(np.ravel_multi_index(move(*at), SIZES))))
    return lax.ppermute(v, AXES, pairs)


def swap_core(v):
    return permute(v, lambda y, zh, c, x, zl: (y, zh, 1 - c, x, zl))


def swap_zh(v):
    return permute(v, lambda y, zh, c, x, zl: (y, 1 - zh, c, x, zl))


def data_target(y, zh, x, zl):
    return (2 * x + zl // 2 - y) % 8, zl % 2


def transpose_data(v):
    def move(y, zh, c, x, zl):
        row_y, row_zh = data_target(y, zh, x, zl)
        return (row_y, row_zh, c, y // 2, 2 * (y % 2) + zh)

    return permute(v, move)


def transpose_in_plane(v, flip):
    def move(y, zh, c, x, zl):
        p = (y - c) % 8
        return (y, zl % 2, c, (p // 2 + x) % 4, 2 * (p % 2 ^ zl // 2) + (zh ^ flip))

    return permute(v, move)


def transpose_along_y(v):
    def move(y, zh, c, x, zl):
        p = (y - c) % 8
        return (2 * ((x - p // 2) % 4) + (p % 2 ^ zl // 2), zh, c, x, zl)

    return permute(v, move)


def pair_swap(v, axis, odd_step, flip=0):
    at = AXES.index(axis)
    n = PARTS[axis]

    def move(*place):
        place = list(place)
        parity = (place[at] - (place[2] ^ flip)) % 2
        step = 1 if parity == odd_step else -1
        place[at] = (place[at] + step) % n
        return tuple(place)

    return permute(v, move)


def take(v, start, size):
    return lax.dynamic_slice_in_dim(v, start, size, 0)


def put(v, part, start):
    return lax.dynamic_update_slice_in_dim(v, part, start, 0)


def in_pair(own, got, odd):
    return jnp.where(odd == 0, jnp.concatenate([own, got]), jnp.concatenate([got, own]))


def scatter_sum(v, axis):
    n = PARTS[axis]
    parts = lax.all_to_all(v.reshape(n, -1, v.shape[1]), axis, 0, 0, tiled=True)
    return jnp.sum(parts, axis=0)


def both_cores(v, c):
    other = swap_core(v)
    out = jnp.zeros((2 * v.shape[0], *v.shape[1:]), v.dtype)
    return put(put(out, v, c * v.shape[0]), other, (1 - c) * v.shape[0])


def together(*parts):
    return lax.optimization_barrier(parts)


def dot(a, b, contract):
    return lax.dot_general(
        a, b, (contract, ((), ())), precision=PREC, preferred_element_type=jnp.float32
    )


def on_device(precision_matrix, sample_rows):
    row_count, col_count = precision_matrix.shape
    samples = sample_rows.shape[1]
    y, zh, c, x, zl = (lax.axis_index(a) for a in AXES)
    row_chip, col_chip = 2 * y + zh, 4 * x + zl
    half = col_count // 2
    block = half // 8
    place = (y - c) % 8
    pair, odd = place // 2, place % 2

    target, _ = data_target(y, zh, x, zl)
    share = take(sample_rows, target * block, block)

    def partial_rows(h):
        cols = lax.dynamic_slice_in_dim(precision_matrix, h * half, half, 1)
        return dot(cols, sample_rows, ((0,), (0,)))

    got = swap_core(partial_rows(1 - c))
    (kept,) = together(partial_rows(c))

    def sums(at):
        start = (at % 4) * (2 * block)
        return take(kept, start, 2 * block) + take(got, start, 2 * block)

    near = jnp.where(odd == 0, pair + 1, pair - 1)
    other = jnp.where(odd == 0, pair - 1, pair + 1)
    sending, share = together(sums(pair + 2), share)
    passed = pair_swap(sending, "y", 1)
    data = transpose_data(share)
    passed = pair_swap(sums(near) + passed, "y", 0)
    sending, data = together(sums(other) + passed, data)
    data_half = lax.all_gather(data, "y", axis=0, tiled=True)
    passed = pair_swap(sending, "y", 1)
    mine = sums(pair) + passed
    passed = pair_swap(take(mine, (1 - odd) * block, block), "y", 0)
    product = take(mine, odd * block, block) + passed
    half_block = block // 2
    parts = [take(product, (zh ^ f) * half_block, half_block) for f in range(2)]
    product, *parts = together(product, *parts)
    moved = [transpose_in_plane(v, f) for f, v in enumerate(parts)]
    zh_got, *moved = together(swap_zh(product), *moved)
    own = moved[0] + moved[1]
    product = product + zh_got
    product_half = lax.all_gather(product, "y", axis=0, tiled=True)
    own = transpose_along_y(own)
    own = lax.all_gather(own, "zl", axis=0, tiled=True)
    own = in_pair(own[:block], own[block:], row_chip // 2 % 2)
    own, data_half = together(own, data_half)
    x_odd = (x - c) % 2
    rows0 = in_pair(own, pair_swap(own, "x", 0), x_odd)
    data_cols = both_cores(data_half, c)
    rows1 = pair_swap(rows0, "x", 1)
    shifted = jnp.concatenate([product_half[block:], product_half[:block]])
    product_cols = both_cores(jnp.where(c == 0, product_half, shifted), c)
    product_rows = jnp.zeros_like(sample_rows)
    first = x - x_odd - row_chip // 4
    for part, at in (
        (rows0[: 2 * block], first),
        (rows0[2 * block :], first + 1),
        (rows1[: 2 * block], first + 2),
        (rows1[2 * block :], first + 3),
    ):
        product_rows = put(product_rows, part, (at % 4) * (2 * block))

    last = ((1,), (1,))
    cross = dot(sample_rows, product_cols, last) + dot(product_rows, data_cols, last)
    gradient = cross * (0.5 / samples)

    global_rows = (2 * row_chip + c) * row_count + lax.broadcasted_iota(
        jnp.int32, (row_count, col_count), 0
    )
    global_cols = col_chip * col_count + lax.broadcasted_iota(
        jnp.int32, (row_count, col_count), 1
    )
    on_diagonal = global_rows == global_cols
    inverse = 1.0 / jnp.where(on_diagonal, precision_matrix, 1.0)
    gradient = gradient - jnp.where(on_diagonal, inverse, 0.0)
    moved = precision_matrix - step_length * gradient
    shrunk = jnp.sign(moved) * jnp.maximum(jnp.abs(moved) - step_length * penalty, 0.0)
    updated = jnp.where(on_diagonal, moved, shrunk)
    next_partial = dot(updated, data_cols, ((1,), (0,)))
    next_product = scatter_sum(scatter_sum(next_partial, "x"), "zl")
    return updated, next_product


def solution(mesh):
    parts = Mesh(mesh.devices.reshape(SIZES), AXES)
    row, col = ("y", "zh", "c"), ("x", "zl")
    return jax.shard_map(
        on_device,
        mesh=parts,
        in_specs=(P(row, col), P(row, None)),
        out_specs=(P(row, col), P(row + col, None)),
        check_vma=False,
    )
```

```python
import jax
import jax.numpy as jnp
import numpy as np
from jax import lax
from jax.sharding import Mesh, PartitionSpec as P

step_length = 0.5
penalty = 0.02

PARTS = {"y": 8, "zh": 2, "c": 2, "x": 4, "zl": 4}
AXES = tuple(PARTS)
SIZES = tuple(PARTS.values())
PREC = lax.Precision.HIGH


def permute(v, move):
    count = int(np.prod(SIZES))
    pairs = []
    for k in range(count):
        at = [int(p) for p in np.unravel_index(k, SIZES)]
        pairs.append((k, int(np.ravel_multi_index(move(*at), SIZES))))
    return lax.ppermute(v, AXES, pairs)


def swap_core(v):
    return permute(v, lambda y, zh, c, x, zl: (y, zh, 1 - c, x, zl))


def swap_zh(v):
    return permute(v, lambda y, zh, c, x, zl: (y, 1 - zh, c, x, zl))


def data_target(y, zh, x, zl):
    return (2 * x + zl // 2 - y) % 8, zl % 2


def transpose_data(v):
    def move(y, zh, c, x, zl):
        row_y, row_zh = data_target(y, zh, x, zl)
        return (row_y, row_zh, c, y // 2, 2 * (y % 2) + zh)

    return permute(v, move)


def transpose_in_plane(v, flip):
    def move(y, zh, c, x, zl):
        p = (y - c) % 8
        return (y, zl % 2, c, (p // 2 + x) % 4, 2 * (p % 2 ^ zl // 2) + (zh ^ flip))

    return permute(v, move)


def transpose_along_y(v):
    def move(y, zh, c, x, zl):
        p = (y - c) % 8
        return (2 * ((x - p // 2) % 4) + (p % 2 ^ zl // 2), zh, c, x, zl)

    return permute(v, move)


def pair_swap(v, axis, odd_step, flip=0):
    at = AXES.index(axis)
    n = PARTS[axis]

    def move(*place):
        place = list(place)
        parity = (place[at] - (place[2] ^ flip)) % 2
        step = 1 if parity == odd_step else -1
        place[at] = (place[at] + step) % n
        return tuple(place)

    return permute(v, move)


def take(v, start, size):
    return lax.dynamic_slice_in_dim(v, start, size, 0)


def put(v, part, start):
    return lax.dynamic_update_slice_in_dim(v, part, start, 0)


def in_pair(own, got, odd):
    return jnp.where(odd == 0, jnp.concatenate([own, got]), jnp.concatenate([got, own]))


def scatter_sum(v, axis):
    n = PARTS[axis]
    parts = lax.all_to_all(v.reshape(n, -1, v.shape[1]), axis, 0, 0, tiled=True)
    return jnp.sum(parts, axis=0)


def both_cores(v, c):
    other = swap_core(v)
    out = jnp.zeros((2 * v.shape[0], *v.shape[1:]), v.dtype)
    return put(put(out, v, c * v.shape[0]), other, (1 - c) * v.shape[0])


def together(*parts):
    return lax.optimization_barrier(parts)


def dot(a, b, contract):
    return lax.dot_general(
        a, b, (contract, ((), ())), precision=PREC, preferred_element_type=jnp.float32
    )


def on_device(precision_matrix, sample_rows):
    row_count, col_count = precision_matrix.shape
    samples = sample_rows.shape[1]
    y, zh, c, x, zl = (lax.axis_index(a) for a in AXES)
    row_chip, col_chip = 2 * y + zh, 4 * x + zl
    half = col_count // 2
    block = half // 8
    place = (y - c) % 8
    pair, odd = place // 2, place % 2

    target, _ = data_target(y, zh, x, zl)
    share = take(sample_rows, target * block, block)

    def partial_rows(h):
        cols = lax.dynamic_slice_in_dim(precision_matrix, h * half, half, 1)
        return dot(cols, sample_rows, ((0,), (0,)))

    got = swap_core(partial_rows(1 - c))
    (kept,) = together(partial_rows(c))

    def sums(at):
        start = (at % 4) * (2 * block)
        return take(kept, start, 2 * block) + take(got, start, 2 * block)

    near = jnp.where(odd == 0, pair + 1, pair - 1)
    other = jnp.where(odd == 0, pair - 1, pair + 1)
    sending, share = together(sums(pair + 2), share)
    passed = pair_swap(sending, "y", 1)
    data = transpose_data(share)
    passed = pair_swap(sums(near) + passed, "y", 0)
    sending = sums(other) + passed
    passed = pair_swap(sending, "y", 1)
    mine = sums(pair) + passed
    passed = pair_swap(take(mine, (1 - odd) * block, block), "y", 0)
    product = take(mine, odd * block, block) + passed
    half_block = block // 2
    parts = [take(product, (zh ^ f) * half_block, half_block) for f in range(2)]
    product, *parts = together(product, *parts)
    moved = [transpose_in_plane(v, f) for f, v in enumerate(parts)]
    zh_got, *moved = together(swap_zh(product), *moved)
    own = moved[0] + moved[1]
    product = product + zh_got
    pieces = lax.all_gather(jnp.stack([product, data]), "y", axis=1, tiled=True)
    own = transpose_along_y(own)
    own = lax.all_gather(own, "zl", axis=0, tiled=True)
    own = in_pair(own[:block], own[block:], row_chip // 2 % 2)
    x_odd = (x - c) % 2
    rows0 = in_pair(own, pair_swap(own, "x", 0), x_odd)
    rows1 = pair_swap(rows0, "x", 1)
    pieces, _ = together(pieces, rows0)
    data_cols = both_cores(pieces[1], c)
    product_half = pieces[0]
    shifted = jnp.concatenate([product_half[block:], product_half[:block]])
    product_cols = both_cores(jnp.where(c == 0, product_half, shifted), c)
    product_rows = jnp.zeros_like(sample_rows)
    first = x - x_odd - row_chip // 4
    for part, at in (
        (rows0[: 2 * block], first),
        (rows0[2 * block :], first + 1),
        (rows1[: 2 * block], first + 2),
        (rows1[2 * block :], first + 3),
    ):
        product_rows = put(product_rows, part, (at % 4) * (2 * block))

    last = ((1,), (1,))
    cross = dot(sample_rows, product_cols, last) + dot(product_rows, data_cols, last)
    gradient = cross * (0.5 / samples)

    global_rows = (2 * row_chip + c) * row_count + lax.broadcasted_iota(
        jnp.int32, (row_count, col_count), 0
    )
    global_cols = col_chip * col_count + lax.broadcasted_iota(
        jnp.int32, (row_count, col_count), 1
    )
    on_diagonal = global_rows == global_cols
    inverse = 1.0 / jnp.where(on_diagonal, precision_matrix, 1.0)
    gradient = gradient - jnp.where(on_diagonal, inverse, 0.0)
    moved = precision_matrix - step_length * gradient
    shrunk = jnp.sign(moved) * jnp.maximum(jnp.abs(moved) - step_length * penalty, 0.0)
    updated = jnp.where(on_diagonal, moved, shrunk)
    next_partial = dot(updated, data_cols, ((1,), (0,)))
    next_product = scatter_sum(scatter_sum(next_partial, "x"), "zl")
    return updated, next_product


def solution(mesh):
    parts = Mesh(mesh.devices.reshape(SIZES), AXES)
    row, col = ("y", "zh", "c"), ("x", "zl")
    return jax.shard_map(
        on_device,
        mesh=parts,
        in_specs=(P(row, col), P(row, None)),
        out_specs=(P(row, col), P(row + col, None)),
        check_vma=False,
    )
```
